32 devices in a mesh: seq: 8 (over z, x), tp: 2 (over y), grp: 2 (over core).
Axes of the slice: x: 2, y: 2, z: 4, core: 2. Of those that a mesh axis runs over, the one named last changes fastest.
Arguments:
- prefill_query: bfloat16 [2, 3072, 8192], P('grp', 'seq', 'tp'), may hold values from -6 to 6
- prefill_keys: bfloat16 [2, 3072, 1024], P('grp', 'seq', 'tp'), may hold values from -6 to 6
- prefill_values: bfloat16 [2, 3072, 1024], P('grp', 'seq', 'tp'), may hold values from -6 to 6
- decode_query: bfloat16 [2, 64, 4, 8192], P('grp', 'seq', None, 'tp'), may hold values from -6 to 6
- decode_keys: bfloat16 [2, 64, 4, 1024], P('grp', 'seq', None, 'tp'), may hold values from -6 to 6
- decode_values: bfloat16 [2, 64, 4, 1024], P('grp', 'seq', None, 'tp'), may hold values from -6 to 6
- page_table: int32 [2, 64, 16], P('grp', 'seq'), may hold values from 0 to 23
- context_lengths: int32 [2, 64], P('grp', 'seq'), may hold values from 1 to 2048
- check_rows: bfloat16 [8, 128], replicated, may hold values from -0.125 to 0.125
Outputs:
- prefill_out: bfloat16 [2, 3072, 8192], P('grp', 'seq', 'tp')
- decode_out: bfloat16 [2, 64, 4, 8192], P('grp', 'seq', None, 'tp')
- page_digest: float32 [2, 64, 8, 2048], P('grp', 'seq', None, 'tp')
The draws below stay inside these ranges and needn't reach their ends.
Inputs may be any that keep to these rules, and one draw needn't show every extreme that they name: page_table[g, r, j] names the page of 128 tokens of prompt 1 - g that holds context tokens j * 128 to j * 128 + 127 of request r; pages may repeat. Request r reads its first context_lengths[g, r] context tokens.
All inputs are finite; a program needn't handle non-finite values.
Results may differ from the reference program's by a relative error of at most 0.014.
Values may be sent and summed in bfloat16 or wider, within the bound.
A program may use at most 128 MiB of HBM per device.

```python
import math
import jax
import jax.numpy as jnp
from jax import lax

HQ = 64
KVH = 8
HD = 128
PAGE = 128
MAXPAGES = 16
STEPS = 4
CSW = 8
PROMPT = 3072
NPAGES = 24
MAXCTX = 2048
REQS = 64


def drawn_normal(key, shape):
    return jax.random.truncated_normal(key, -6.0, 6.0, shape, jnp.float32)


def draw_prefill_query(key, part):
    values = drawn_normal(jax.random.fold_in(key, 11), (2, PROMPT, HQ * HD))
    return values.astype(jnp.bfloat16)


def draw_prefill_keys(key, part):
    values = drawn_normal(jax.random.fold_in(key, 12), (2, PROMPT, KVH * HD))
    return values.astype(jnp.bfloat16)


def draw_decode_query(key, part):
    values = drawn_normal(jax.random.fold_in(key, 13), (2, REQS, STEPS, HQ * HD))
    return values.astype(jnp.bfloat16)


def draw_decode_keys(key, part):
    values = drawn_normal(jax.random.fold_in(key, 14), (2, REQS, STEPS, KVH * HD))
    return values.astype(jnp.bfloat16)


def touch_ends(result, stream_key, low, high):
    shape = result.shape
    index_at = [jax.random.randint(jax.random.fold_in(stream_key, axis), (), 0, shape[axis]) for axis in range(len(shape))]
    result = result.at[tuple(index_at)].set(low)
    longest = shape.index(max(shape))
    index_at[longest] = (index_at[longest] + 1) % shape[longest]
    return result.at[tuple(index_at)].set(high)


def steps_of(own_key, dims, split, least, high):
    def one(position, shards_of):
        heights = jax.random.uniform(jax.random.fold_in(jax.random.fold_in(own_key, 6), position), (shards_of,), jnp.float32, least / len(split), high / len(split))
        return jnp.repeat(jnp.exp(heights), dims[position] // shards_of).reshape((-1,) + (1,) * (len(dims) - position - 1))

    factor_of = one(*split[0])
    for cut in split[1:]:
        factor_of = factor_of * one(*cut)
    return factor_of


def bell_draw(stream_key, extent, deviation, reach, split=(), kind=jnp.bfloat16):
    level = steps_of(stream_key, extent, split, -0.22, 0.18) if split else 1.0
    values = jax.random.normal(stream_key, extent, jnp.float32) * deviation * level
    return jnp.minimum(jnp.maximum(values, -reach), reach).astype(kind)


def setup_inputs(seed: int = 0) -> dict:
    streams_of = jax.random.split(jax.random.key(seed), 10)
    return {
        "prefill_query": draw_prefill_query(jax.random.fold_in(streams_of[9], 71), 0),
        "prefill_keys": draw_prefill_keys(jax.random.fold_in(streams_of[9], 71), 0),
        "prefill_values": bell_draw(streams_of[2], (2, PROMPT, KVH * HD), 1.0, 6.0, ((0, 2), (1, 8), (2, 2))),
        "decode_query": draw_decode_query(jax.random.fold_in(streams_of[9], 71), 0),
        "decode_keys": draw_decode_keys(jax.random.fold_in(streams_of[9], 71), 0),
        "decode_values": bell_draw(streams_of[5], (2, REQS, STEPS, KVH * HD), 1.0, 6.0, ((0, 2), (1, 8), (3, 2))),
        "page_table": touch_ends(jax.random.randint(streams_of[6], (2, REQS, MAXPAGES), 0, NPAGES), jax.random.fold_in(streams_of[6], 1), 0, NPAGES - 1).astype(jnp.int32),
        "context_lengths": touch_ends(jax.random.randint(streams_of[7], (2, REQS), 1, MAXCTX + 1), jax.random.fold_in(streams_of[7], 1), 1, MAXCTX).astype(jnp.int32),
        "check_rows": bell_draw(streams_of[8], (CSW, PAGE), MAXCTX ** -0.5, 0.125),
    }


def rounded(weights):
    return lax.optimization_barrier(weights.astype(jnp.bfloat16)).astype(jnp.float32)

def prompt_attention(query_rows, key_rows, value_rows):
    groups = HQ // KVH
    block_rows = math.gcd(128, PROMPT)
    score_scale = 1.0 / math.sqrt(HD)
    blocks = query_rows.reshape(PROMPT // block_rows, block_rows, KVH, groups, HD)
    key_heads = key_rows.reshape(PROMPT, KVH, HD).astype(jnp.float32)
    value_heads = value_rows.reshape(PROMPT, KVH, HD).astype(jnp.float32)
    columns = jnp.arange(PROMPT, dtype=jnp.int32)

    def one_block(block_pair):
        query_block, block_index = block_pair
        scores = jnp.einsum('rkgd,ckd->kgrc', query_block.astype(jnp.float32), key_heads) * score_scale
        places = block_index * block_rows + jnp.arange(block_rows, dtype=jnp.int32)
        allowed = columns[None, :] <= places[:, None]
        scores = jnp.where(allowed, scores, -jnp.inf)
        row_max = lax.optimization_barrier(jnp.max(scores, axis=-1, keepdims=True))
        weights = jnp.where(allowed, jnp.exp(scores - row_max), 0.0)
        row_total = lax.optimization_barrier(jnp.sum(weights, axis=-1))
        mixed = jnp.einsum('kgrc,ckd->rkgd', rounded(weights), value_heads)
        mixed = mixed / jnp.transpose(row_total, (2, 0, 1))[..., None]
        return mixed.reshape(block_rows, HQ * HD).astype(jnp.bfloat16)
    outputs = lax.map(one_block, (blocks, jnp.arange(PROMPT // block_rows, dtype=jnp.int32)))
    return outputs.reshape(PROMPT, HQ * HD)

def decode_group(query, new_keys, new_values, own_table, lengths, key_rows, value_rows, check_rows):
    groups = HQ // KVH
    score_scale = 1.0 / math.sqrt(HD)
    offsets = jnp.arange(PAGE, dtype=jnp.int32)
    positions = jnp.arange(MAXCTX, dtype=jnp.int32)
    step_order = jnp.arange(STEPS, dtype=jnp.int32)
    causal = step_order[None, :] <= step_order[:, None]
    check_full = jnp.tile(check_rows.astype(jnp.float32), (1, MAXPAGES))

    def one_request(request_items):
        query_rows, fresh_keys, fresh_values, table_row, length = request_items
        token_index = (table_row[:, None] * PAGE + offsets[None, :]).reshape(MAXCTX).astype(jnp.int32)
        context_keys = key_rows[token_index].reshape(MAXCTX, KVH, HD).astype(jnp.float32)
        context_values = value_rows[token_index].reshape(MAXCTX, KVH, HD).astype(jnp.float32)
        live = positions < length
        query_heads = query_rows.reshape(STEPS, KVH, groups, HD).astype(jnp.float32)
        old_scores = jnp.einsum('skgd,tkd->skgt', query_heads, context_keys) * score_scale
        old_scores = jnp.where(live[None, None, None, :], old_scores, -jnp.inf)
        fresh_heads = fresh_keys.reshape(STEPS, KVH, HD).astype(jnp.float32)
        fresh_scores = jnp.einsum('skgd,jkd->skgj', query_heads, fresh_heads) * score_scale
        fresh_scores = jnp.where(causal[:, None, None, :], fresh_scores, -jnp.inf)
        joint_max = jnp.maximum(lax.optimization_barrier(jnp.max(old_scores, axis=-1)), lax.optimization_barrier(jnp.max(fresh_scores, axis=-1)))[..., None]
        old_weights = jnp.where(live[None, None, None, :], jnp.exp(old_scores - joint_max), 0.0)
        fresh_weights = jnp.where(causal[:, None, None, :], jnp.exp(fresh_scores - joint_max), 0.0)
        totals = lax.optimization_barrier(jnp.sum(old_weights, axis=-1)) + lax.optimization_barrier(jnp.sum(fresh_weights, axis=-1))
        mixed = jnp.einsum('skgt,tkd->skgd', rounded(old_weights), context_values)
        fresh_value_heads = fresh_values.reshape(STEPS, KVH, HD).astype(jnp.float32)
        mixed = mixed + jnp.einsum('skgj,jkd->skgd', rounded(fresh_weights), fresh_value_heads)
        output = (mixed / totals[..., None]).reshape(STEPS, HQ * HD).astype(jnp.bfloat16)
        check_live = check_full * live[None, :].astype(jnp.float32)
        paired = jnp.concatenate([context_keys, context_values], axis=-1)
        digest = jnp.einsum('ct,tke->cke', check_live, paired, precision=lax.Precision.HIGHEST)
        return (output, digest.reshape(CSW, KVH * 2 * HD))
    return lax.map(one_request, (query, new_keys, new_values, own_table, lengths))

def reference(prefill_query, prefill_keys, prefill_values, decode_query, decode_keys, decode_values, page_table, context_lengths, check_rows):
    prefill_out = jnp.stack([prompt_attention(prefill_query[0], prefill_keys[0], prefill_values[0]), prompt_attention(prefill_query[1], prefill_keys[1], prefill_values[1])])
    outputs = []
    digests = []
    for group in range(2):
        output, digest = decode_group(decode_query[group], decode_keys[group], decode_values[group], page_table[group], context_lengths[group], prefill_keys[1 - group], prefill_values[1 - group], check_rows)
        outputs.append(output)
        digests.append(digest)
    return (prefill_out, jnp.stack(outputs), jnp.stack(digests))
```

```python
import functools
import math

import jax
import jax.numpy as jnp
from jax import lax
from jax.experimental import pallas as pl
from jax.experimental.pallas import tpu as pltpu
from jax.sharding import PartitionSpec as P

HQ = 64
KVH = 8
HD = 128
PAGE = 128
GROUPS = HQ // KVH

neg_large = -1e30
SCALE2 = math.log2(math.e) / math.sqrt(HD)
NT = (((1,), (1,)), ((), ()))


def partner(shard, axis):
    return lax.ppermute(shard, axis, [(i, i ^ 1) for i in range(lax.axis_size(axis))])


def fold(q_ref, keys, values_t, g, mask, max_ref, total_ref, sum_ref, first):
    scores = lax.dot_general(
        keys, q_ref[:, g * HD : (g + 1) * HD], NT, preferred_element_type=jnp.float32
    ) * SCALE2
    if mask is not None:
        scores = jnp.where(mask, scores, neg_large)
    highest = jnp.max(scores, axis=0, keepdims=True)
    if not first:
        old_max = max_ref[g]
        highest = jnp.maximum(highest, old_max)
    weights = jnp.exp2(scores - highest)
    totals = jnp.sum(weights, axis=0, keepdims=True)
    update = jnp.dot(values_t, weights.astype(jnp.bfloat16), preferred_element_type=jnp.float32)
    if not first:
        fading = jnp.exp2(old_max - highest)
        totals = totals + total_ref[g] * fading
        update = update + sum_ref[g] * fading
    max_ref[g] = highest
    total_ref[g] = totals
    sum_ref[g] = update


def head_kernel(
    steps,
    members,
    owners_ref,
    q_ref,
    *refs,
):
    piece_refs = refs[:members]
    dq_ref, fresh_ref, counts_ref, checks_ref, out_ref, dout_ref, digest_ref = refs[members:-4]
    max_ref, total_ref, sum_ref, kv_ref = refs[-4:]
    rows = q_ref.shape[0]
    for c in range(members):
        kv_ref[c * rows : (c + 1) * rows] = piece_refs[c][...]
    row = lax.broadcasted_iota(jnp.int32, (rows, rows), 0)
    col = lax.broadcasted_iota(jnp.int32, (rows, rows), 1)
    own = kv_ref[:rows]
    own_t = own[:, HD:].T
    for g in range(GROUPS):
        fold(q_ref, own[:, :HD], own_t, g, row <= col, max_ref, total_ref, sum_ref, True)

    def advance(c, carry):
        @pl.when(owners_ref[c] < owners_ref[0])
        def _():
            kv = kv_ref[pl.ds(pl.multiple_of(c * rows, rows), rows)]
            kv_t = kv[:, HD:].T
            for g in range(GROUPS):
                fold(q_ref, kv[:, :HD], kv_t, g, None, max_ref, total_ref, sum_ref, False)

        return carry

    lax.fori_loop(1, members, advance, 0)
    for g in range(GROUPS):
        out_ref[:, g * HD : (g + 1) * HD] = (sum_ref[g] / total_ref[g]).T.astype(jnp.bfloat16)

    requests, tokens = counts_ref.shape
    asked = dq_ref.shape[0]
    per = asked // requests
    dq = dq_ref[...]
    counts = jnp.broadcast_to(counts_ref[...][:, None, :], (requests, per, tokens)).reshape(
        asked, tokens
    )
    scores = lax.dot_general(dq, kv_ref[:, :HD], NT, preferred_element_type=jnp.float32) * SCALE2
    live = counts > 0
    scores = jnp.where(live, scores, neg_large)
    fresh = fresh_ref[...]
    count_fresh = fresh.shape[0]
    fresh_scores = lax.dot_general(
        dq, fresh[:, :HD], NT, preferred_element_type=jnp.float32
    ) * SCALE2
    drow = lax.broadcasted_iota(jnp.int32, (asked, count_fresh), 0)
    dcol = lax.broadcasted_iota(jnp.int32, (asked, count_fresh), 1)
    allowed = (drow // per == dcol // steps) & (dcol % steps <= (drow % per) // GROUPS)
    fresh_scores = jnp.where(allowed, fresh_scores, neg_large)
    highest = jnp.maximum(
        jnp.max(scores, axis=1, keepdims=True), jnp.max(fresh_scores, axis=1, keepdims=True)
    )
    weights = jnp.exp2(scores - highest)
    fresh_weights = jnp.exp2(fresh_scores - highest)
    totals = jnp.sum(weights * counts, axis=1, keepdims=True) + jnp.sum(
        fresh_weights, axis=1, keepdims=True
    )
    weighted = (weights.astype(jnp.bfloat16).astype(jnp.float32) * counts).astype(jnp.bfloat16)
    summed = jnp.dot(weighted, kv_ref[:, HD:], preferred_element_type=jnp.float32)
    summed = summed + jnp.dot(
        fresh_weights.astype(jnp.bfloat16), fresh[:, HD:], preferred_element_type=jnp.float32
    )
    dout_ref[...] = (summed / totals).astype(jnp.bfloat16)
    both = jnp.dot(checks_ref[...], kv_ref[...], preferred_element_type=jnp.float32)
    half = both.shape[0] // 2
    digest_ref[...] = both[:half] + both[half:]


def one_head(head, steps, owners, query, pieces, dq, fresh, counts, checks):
    rows = query.shape[0]
    members = len(pieces)
    tokens = members * rows
    asked = dq.shape[1]
    whole = lambda a: pl.BlockSpec(a.shape, lambda i: (0,) * a.ndim)
    return pl.pallas_call(
        functools.partial(head_kernel, steps, members),
        grid=(1,),
        in_specs=[
            pl.BlockSpec(memory_space=pltpu.SMEM),
            pl.BlockSpec((rows, GROUPS * HD), lambda i: (0, head)),
            *[whole(piece) for piece in pieces],
            pl.BlockSpec((None, asked, HD), lambda i: (head, 0, 0)),
            pl.BlockSpec((None,) + fresh.shape[1:], lambda i: (head, 0, 0)),
            whole(counts),
            whole(checks),
        ],
        out_specs=[
            pl.BlockSpec((rows, GROUPS * HD), lambda i: (0, 0)),
            pl.BlockSpec((asked, HD), lambda i: (0, 0)),
            pl.BlockSpec((checks.shape[0] // 2, 2 * HD), lambda i: (0, 0)),
        ],
        out_shape=[
            jax.ShapeDtypeStruct((rows, GROUPS * HD), jnp.bfloat16),
            jax.ShapeDtypeStruct((asked, HD), jnp.bfloat16),
            jax.ShapeDtypeStruct((checks.shape[0] // 2, 2 * HD), jnp.float32),
        ],
        scratch_shapes=[
            pltpu.VMEM((GROUPS, 1, rows), jnp.float32),
            pltpu.VMEM((GROUPS, 1, rows), jnp.float32),
            pltpu.VMEM((GROUPS, HD, rows), jnp.float32),
            pltpu.VMEM((tokens, 2 * HD), jnp.bfloat16),
        ],
        compiler_params=pltpu.CompilerParams(vmem_limit_bytes=44 * 1024 * 1024),
        cost_estimate=pl.CostEstimate(
            flops=4 * rows * tokens * HD * GROUPS * 3,
            bytes_accessed=4 * rows * GROUPS * HD + 4 * tokens * HD,
            transcendentals=rows * tokens * GROUPS,
        ),
    )(owners, query, *pieces, dq, fresh, counts, checks)


def shards(
    prefill_query,
    prefill_keys,
    prefill_values,
    decode_query,
    decode_keys,
    decode_values,
    page_table,
    context_lengths,
    check_rows,
):
    key_rows = prefill_keys[0]
    value_rows = prefill_values[0]
    row_count = key_rows.shape[0]
    kv_local = key_rows.shape[1] // HD
    members = lax.axis_size("seq")
    me = lax.axis_index("seq")
    requests, step_count = decode_query.shape[1:3]
    asked = requests * step_count * GROUPS

    shifts = list(range(0, members, 2))
    line = [(me - s) % members for s in shifts]
    owners = jnp.stack(line + [((me ^ 1) - s) % members for s in shifts]).astype(jnp.int32)

    dq, dk, dv, table, lengths = partner(
        (decode_query[0], decode_keys[0], decode_values[0], page_table[0], context_lengths[0]),
        "grp",
    )
    dq = dq.reshape(requests, step_count, kv_local, GROUPS, HD)
    dq = jnp.transpose(dq, (2, 0, 1, 3, 4)).reshape(kv_local, asked, HD)
    fresh = jnp.concatenate(
        [a.reshape(requests * step_count, kv_local, HD) for a in (dk, dv)], axis=-1
    )
    fresh = jnp.transpose(fresh, (1, 0, 2))
    own_pages = row_count // PAGE
    max_pages = table.shape[1]
    page_ids = (owners[:, None] * own_pages + jnp.arange(own_pages, dtype=jnp.int32)).reshape(-1)
    hits = (table[:, :, None] == page_ids[None, None, :]).astype(jnp.float32)
    place = jnp.arange(max_pages * PAGE, dtype=jnp.int32).reshape(max_pages, PAGE)
    fits = (place[None] < lengths[:, None, None]).astype(jnp.float32)
    counts = jnp.einsum("ajp,ajo->apo", hits, fits)
    checks = counts[:, None] * check_rows.astype(jnp.float32)[None, :, None, :]
    counts = counts.reshape(requests, -1)
    check_count = check_rows.shape[0]
    checks = checks.reshape(requests * check_count, -1)
    upper = checks.astype(jnp.bfloat16)
    lower = (checks - upper.astype(jnp.float32)).astype(jnp.bfloat16)
    checks = jnp.concatenate([upper, lower], axis=0)

    pieces = []
    for h in range(kv_local):
        cut = slice(h * HD, (h + 1) * HD)
        own = jnp.concatenate([key_rows[:, cut], value_rows[:, cut]], axis=1)
        if h >= 2:
            pieces[h - 2], own = lax.optimization_barrier((pieces[h - 2], own))
        got = [own] + [
            lax.ppermute(own, "seq", [(i, (i + s) % members) for i in range(members)])
            for s in shifts[1:]
        ]
        pieces.append(got + [partner(b, "seq") for b in got])

    outs, douts, digests = [], [], []
    for h in range(kv_local):
        if h >= 1:
            pieces[h], outs[h - 1] = lax.optimization_barrier((pieces[h], outs[h - 1]))
        out, dout, digest = one_head(
            h, step_count, owners, prefill_query[0], pieces[h], dq, fresh, counts, checks
        )
        outs.append(out)
        douts.append(dout)
        digests.append(digest)
    prefill_out = jnp.concatenate(outs, axis=1)[None]
    dout = jnp.stack(douts, axis=0).reshape(kv_local, requests, step_count, GROUPS * HD)
    digest = jnp.stack(digests, axis=0).reshape(kv_local, requests, check_count, 2 * HD)
    dout, digest = partner((dout, digest), "grp")
    decode_out = jnp.transpose(dout, (1, 2, 0, 3)).reshape(requests, step_count, -1)[None]
    page_digest = jnp.transpose(digest, (1, 2, 0, 3)).reshape(requests, check_count, -1)[None]
    return (prefill_out, decode_out, page_digest)


def solution(mesh):
    in_specs = (
        P("grp", "seq", "tp"),
        P("grp", "seq", "tp"),
        P("grp", "seq", "tp"),
        P("grp", "seq", None, "tp"),
        P("grp", "seq", None, "tp"),
        P("grp", "seq", None, "tp"),
        P("grp", "seq", None),
        P("grp", "seq"),
        P(),
    )
    out_specs = (P("grp", "seq", "tp"), P("grp", "seq", None, "tp"), P("grp", "seq", None, "tp"))
    return jax.shard_map(shards, mesh=mesh, in_specs=in_specs, out_specs=out_specs, check_vma=False)
```
